32 devices in a mesh: rep: 4 (over x, core), gx: 2 (over y), gy: 4 (over z).
Axes of the slice: x: 2, y: 2, z: 4, core: 2. Of those that a mesh axis runs over, the one named last changes fastest.
Arguments:
- node_feat: bfloat16 [8192, 256], P(('rep', 'gx', 'gy')), may hold values from -6 to 6
- edge_feat: bfloat16 [262144, 256], P(('rep', 'gx', 'gy')), may hold values from -6 to 6
- edge_src: int32 [262144], P(('rep', 'gx', 'gy')), may hold values from 0 to 1023
- edge_dst: int32 [262144], P(('rep', 'gx', 'gy')), may hold values from 0 to 255
- edge_count: int32 [32], P(('rep', 'gx', 'gy')), may hold values from 2048 to 8192, as said below
- send_idx: int32 [4, 2, 4, 2, 2, 64], P('rep', 'gx', 'gy'), may hold values from 0 to 255
- w_qkv: bfloat16 [2, 256, 768], replicated, may hold values from -0.375 to 0.375
- w_edge: bfloat16 [2, 256, 256], replicated, may hold values from -0.375 to 0.375
- gains: float32 [2, 256], replicated, may hold values from 0.1 to 1.9
- head_in: bfloat16 [256, 256], replicated, may hold values from -0.375 to 0.375
- head_out: bfloat16 [256, 169], replicated, may hold values from -0.375 to 0.375
- targets: bfloat16 [169, 262144], P(None, ('rep', 'gx', 'gy')), may hold values from -15 to 15
Outputs:
- node_out: bfloat16 [8192, 256], P(('rep', 'gx', 'gy'))
- grad_head_in: float32 [256, 256], replicated
- grad_head_out: float32 [256, 169], replicated
The draws below stay inside these ranges and needn't reach their ends.
Inputs may be any that keep to these rules, and one draw needn't show every extreme that they name: `edge_count`: edge slots of a tile at positions from its count on are padding; some tile holds 8192 live edges.
All inputs are finite; a program needn't handle non-finite values.
Results may differ from the reference program's by a relative error of at most 0.0025.
The reference program's roundings to bfloat16 on the way count: a program that leaves them out, or rounds other values in their place, can miss the bound.
Values may be sent and summed in bfloat16 or wider, within the bound.
A program may use at most 128 MiB of HBM per device.

```python
import jax
import jax.numpy as jnp
from jax import lax

HIDDEN_SIZE = 256
ORB2 = 169
LAYERS = 2
GHOST_CELL = 64
ATOM_DEV = 256
EDGE_DEV = 8192
DEVS = 32
ATOMS = 8192
EDGES = 262144
TABLE = 1024
N_REP = 4
N_GX = 2
N_GY = 4


def draw_edge_count(key, part):
    first_key, second_key = jax.random.split(jax.random.fold_in(key, 17))
    counts = jax.random.randint(first_key, (DEVS,), EDGE_DEV // 4, EDGE_DEV + 1)
    fullest = jax.random.randint(second_key, (), 0, DEVS)
    return jnp.where(jnp.arange(DEVS) == fullest, EDGE_DEV, counts).astype(jnp.int32)


def plant(array, own_key, low, largest):
    extent = array.shape
    index_at = [jax.random.randint(jax.random.fold_in(own_key, axis), (), 0, extent[axis]) for axis in range(len(extent))]
    array = array.at[tuple(index_at)].set(low)
    longest = extent.index(max(extent))
    index_at[longest] = (index_at[longest] + 1) % extent[longest]
    return array.at[tuple(index_at)].set(largest)


def block_scale(key, shape, cuts, low, largest):
    def one(position, shards_of):
        draws = jax.random.uniform(jax.random.fold_in(jax.random.fold_in(key, 6), position), (shards_of,), jnp.float32, low / len(cuts), largest / len(cuts))
        return jnp.repeat(jnp.exp(draws), shape[position] // shards_of).reshape((-1,) + (1,) * (len(shape) - position - 1))

    factor_of = one(*cuts[0])
    for cut in cuts[1:]:
        factor_of = factor_of * one(*cut)
    return factor_of


def centred(key, dims, deviation, reach, cuts=(), held_as=jnp.bfloat16):
    result = deviation * jax.random.normal(key, dims, jnp.float32)
    if cuts:
        result = result * block_scale(key, dims, cuts, -0.22, 0.18)
    return jnp.clip(result, -reach, reach).astype(held_as)


def setup_inputs(seed: int = 0) -> dict:
    streams_of = jax.random.split(jax.random.key(seed), 13)
    node_feat = centred(streams_of[0], (ATOMS, HIDDEN_SIZE), 1.0, 6.0, ((0, 32),))
    edge_feat = centred(streams_of[1], (EDGES, HIDDEN_SIZE), 1.0, 6.0, ((0, 32),))
    edge_src = plant(jax.random.randint(streams_of[2], (EDGES,), 0, TABLE), jax.random.fold_in(streams_of[2], 1), 0, TABLE - 1).astype(jnp.int32)
    edge_dst = plant(jax.random.randint(streams_of[3], (EDGES,), 0, ATOM_DEV), jax.random.fold_in(streams_of[3], 1), 0, ATOM_DEV - 1).astype(jnp.int32)
    edge_count = draw_edge_count(jax.random.fold_in(streams_of[12], 71), 0)
    send_idx = plant(jax.random.randint(streams_of[5], (N_REP, N_GX, N_GY, 2, 2, GHOST_CELL), 0, ATOM_DEV), jax.random.fold_in(streams_of[5], 1), 0, ATOM_DEV - 1).astype(jnp.int32)
    w_qkv = centred(streams_of[6], (LAYERS, HIDDEN_SIZE, 3 * HIDDEN_SIZE), HIDDEN_SIZE ** -0.5, 0.375)
    w_edge = centred(streams_of[7], (LAYERS, HIDDEN_SIZE, HIDDEN_SIZE), HIDDEN_SIZE ** -0.5, 0.375)
    gains = jnp.clip(1.0 + 0.18 * jax.random.normal(streams_of[8], (LAYERS, HIDDEN_SIZE), jnp.float32), 0.1, 1.9)
    head_in = centred(streams_of[9], (HIDDEN_SIZE, HIDDEN_SIZE), HIDDEN_SIZE ** -0.5, 0.375)
    head_out = centred(streams_of[10], (HIDDEN_SIZE, ORB2), HIDDEN_SIZE ** -0.5, 0.375)
    targets = centred(streams_of[11], (ORB2, EDGES), 2.5, 15.0, ((1, 32),))
    return {"node_feat": node_feat, "edge_feat": edge_feat, "edge_src": edge_src, "edge_dst": edge_dst, "edge_count": edge_count, "send_idx": send_idx, "w_qkv": w_qkv, "w_edge": w_edge, "gains": gains, "head_in": head_in, "head_out": head_out, "targets": targets}


OUTER_CELLS = ((0, 0), (0, 1), (0, 2), (0, 3), (1, 0), (1, 3), (2, 0), (2, 3), (3, 0), (3, 1), (3, 2), (3, 3))
CELL_SOURCE = ((-1, 1), (0, 0), (0, 1), (1, 0))

def layer_norm(values):
    centre = values - lax.optimization_barrier(jnp.mean(values, axis=-1, keepdims=True))
    spread = lax.optimization_barrier(jnp.mean(centre * centre, axis=-1, keepdims=True))
    return centre * lax.rsqrt(spread + 1e-05)

def build_ghosts(nodes, send_idx):
    flat_nodes = nodes.reshape(DEVS, ATOM_DEV, HIDDEN_SIZE)
    flat_index = send_idx.reshape(DEVS, 4 * GHOST_CELL).astype(jnp.int32)
    buffers = jax.vmap(lambda rows, picks: rows[picks])(flat_nodes, flat_index)
    buffers = buffers.reshape(N_REP, N_GX, N_GY, 2, 2, GHOST_CELL, HIDDEN_SIZE)
    slabs = []
    for cell_i, cell_j in OUTER_CELLS:
        offset_x, half_x = CELL_SOURCE[cell_i]
        offset_y, half_y = CELL_SOURCE[cell_j]
        slab = buffers[:, :, :, half_x, half_y]
        slab = jnp.roll(slab, shift=(-offset_x, -offset_y), axis=(1, 2))
        slabs.append(slab)
    ghosts = jnp.concatenate(slabs, axis=3)
    return ghosts.reshape(DEVS, 12 * GHOST_CELL, HIDDEN_SIZE)

def tile_layer(nodes, ghosts, edges, sources, receivers, live, weight_qkv, weight_edge, gain_row):
    projected = jnp.dot(nodes, weight_qkv, preferred_element_type=jnp.float32).astype(jnp.bfloat16)
    ghost_kv = jnp.dot(ghosts, weight_qkv[:, HIDDEN_SIZE:], preferred_element_type=jnp.float32).astype(jnp.bfloat16)
    table = jnp.concatenate([projected[:, HIDDEN_SIZE:], ghost_kv], axis=0)
    gathered = table[sources]
    queries = projected[:, :HIDDEN_SIZE][receivers]
    pre_act = queries.astype(jnp.float32) + gathered[:, :HIDDEN_SIZE].astype(jnp.float32)
    pre_act = pre_act + jnp.dot(edges, weight_edge, preferred_element_type=jnp.float32)
    new_edges = (edges.astype(jnp.float32) + live * jax.nn.silu(pre_act)).astype(jnp.bfloat16)
    weighted = live * jax.nn.sigmoid(pre_act) * gathered[:, HIDDEN_SIZE:].astype(jnp.float32)
    summed = jax.ops.segment_sum(weighted, receivers, num_segments=ATOM_DEV)
    new_nodes = (nodes.astype(jnp.float32) + gain_row * layer_norm(summed)).astype(jnp.bfloat16)
    return (new_nodes, new_edges)

def tile_readout(edges, live_row, target_block, head_in, head_out):
    scale = 0.125 / (EDGE_DEV * DEVS) ** 0.5
    act_in = jnp.dot(edges, head_in, preferred_element_type=jnp.float32)
    hidden_head = jax.nn.silu(act_in).astype(jnp.bfloat16)
    pred = lax.dot_general(head_out, hidden_head, (((0,), (1,)), ((), ())), preferred_element_type=jnp.float32)
    dpred = (live_row * (pred - target_block.astype(jnp.float32)) * scale).astype(jnp.bfloat16)
    dhidden = lax.dot_general(dpred, head_out, (((0,), (1,)), ((), ())), preferred_element_type=jnp.float32)
    sig = jax.nn.sigmoid(act_in)
    dact = (dhidden * sig * (1.0 + act_in * (1.0 - sig))).astype(jnp.bfloat16)
    grad_in = lax.dot_general(edges, dact, (((0,), (0,)), ((), ())), preferred_element_type=jnp.float32)
    grad_out = lax.dot_general(hidden_head, dpred, (((0,), (1,)), ((), ())), preferred_element_type=jnp.float32)
    return (grad_in, grad_out)

def reference(node_feat, edge_feat, edge_src, edge_dst, edge_count, send_idx, w_qkv, w_edge, gains, head_in, head_out, targets):
    nodes = node_feat.reshape(DEVS, ATOM_DEV, HIDDEN_SIZE)
    edges = edge_feat.reshape(DEVS, EDGE_DEV, HIDDEN_SIZE)
    sources = edge_src.reshape(DEVS, EDGE_DEV).astype(jnp.int32)
    receivers = edge_dst.reshape(DEVS, EDGE_DEV).astype(jnp.int32)
    positions = jnp.arange(EDGE_DEV, dtype=jnp.int32)
    live = (positions[None, :] < edge_count[:, None]).astype(jnp.float32)[:, :, None]
    for layer_index in range(LAYERS):
        ghosts = build_ghosts(nodes, send_idx)
        weight_qkv = w_qkv[layer_index]
        weight_edge = w_edge[layer_index]
        gain_row = gains[layer_index]

        def one_tile(items):
            return tile_layer(items[0], items[1], items[2], items[3], items[4], items[5], weight_qkv, weight_edge, gain_row)
        nodes, edges = lax.map(one_tile, (nodes, ghosts, edges, sources, receivers, live))
    target_tiles = jnp.transpose(targets.reshape(ORB2, DEVS, EDGE_DEV), (1, 0, 2))
    live_rows = live[:, :, 0][:, None, :]

    def readout(items):
        return tile_readout(items[0], items[1], items[2], head_in, head_out)
    grad_in, grad_out = lax.map(readout, (edges, live_rows, target_tiles))
    return (nodes.reshape(ATOMS, HIDDEN_SIZE), lax.optimization_barrier(jnp.sum(grad_in, axis=0)), lax.optimization_barrier(jnp.sum(grad_out, axis=0)))
```

```python
import functools

import jax
import jax.numpy as jnp
from jax import lax
from jax.experimental import pallas as pl
from jax.experimental.pallas import tpu as pltpu
from jax.sharding import PartitionSpec as P

F32 = jnp.float32
BF16 = jnp.bfloat16
BLOCK = 1024
SUB = 512
CELLS = tuple((i, j) for i in range(4) for j in range(4) if not (i in (1, 2) and j in (1, 2)))
NT = (((1,), (1,)), ((), ()))


def nn(a, b):
    return jnp.dot(a, b, preferred_element_type=F32)


def nt(a, b):
    return lax.dot_general(a, b, NT, preferred_element_type=F32)


def sigmoid(v):
    return 0.5 * jnp.tanh(0.5 * v) + 0.5


def hot(rows_iota, row, base):
    picked = jnp.where((row >= base) & (row < base + 256), row - base, -1)
    picked = picked.astype(F32).astype(BF16)
    return jnp.where(rows_iota == picked, jnp.ones((), BF16), jnp.zeros((), BF16))


def fill_tables(nodes, ghosts, w_qkv, kv_t, q_t):
    atoms = nodes.shape[0]
    w_t = w_qkv.T
    q_t[...] = nt(w_t[:256], nodes).astype(BF16)
    kv_t[:, :atoms] = nt(w_t[256:], nodes).astype(BF16)
    kv_t[:, atoms:] = nt(w_t[256:], ghosts).astype(BF16)


def edge_step(edges_t, src, dst, live, iota, kv_t, q_t, we_t):
    dst_hot = hot(iota, dst, 0)
    table_rows = kv_t.shape[1]
    gathered = nn(kv_t[:, :256], hot(iota, src, 0))
    for base in range(256, table_rows, 256):
        gathered = gathered + nn(kv_t[:, base : base + 256], hot(iota, src, base))
    pre = gathered[:256] + nn(q_t[...], dst_hot) + nn(we_t[...], edges_t)
    gate = live * sigmoid(pre)
    new_edges = (edges_t.astype(F32) + gate * pre).astype(BF16)
    weighted = gate * gathered[256:]
    high = weighted.astype(BF16)
    low = (weighted - high.astype(F32)).astype(BF16)
    added = nt(jnp.concatenate([high, low], axis=0), dst_hot)
    return new_edges, added[:256] + added[256:]


def update_nodes(nodes, summed_t, gain):
    summed = summed_t.T
    centre = summed - jnp.mean(summed, axis=-1, keepdims=True)
    spread = jnp.mean(centre * centre, axis=-1, keepdims=True)
    return (nodes.astype(F32) + gain * (centre * lax.rsqrt(spread + 1e-05))).astype(BF16)


def layer_kernel(
    layer, scale, count, nodes, ghosts, w_qkv, w_edge, gains, edges, src, dst, *rest
):
    last = scale is not None
    if last:
        head_in, head_out, targets, out_nodes, grad_in, grad_out = rest[:6]
        kv_t, q_t, we_t, iota, summed, head_in_t, head_out_t = rest[6:]
    else:
        out_nodes, out_edges = rest[:2]
        kv_t, q_t, we_t, iota, summed = rest[2:]
    step = pl.program_id(0)

    @pl.when(step == 0)
    def _():
        fill_tables(nodes[...], ghosts[...], w_qkv[0], kv_t, q_t)
        we_t[...] = w_edge[0].T
        iota[...] = lax.broadcasted_iota(jnp.int32, iota.shape, 0).astype(F32).astype(BF16)
        summed[...] = jnp.zeros_like(summed)
        if last:
            head_in_t[...] = head_in[...].T
            head_out_t[...] = head_out[...].T
            grad_in[...] = jnp.zeros_like(grad_in)
            grad_out[...] = jnp.zeros_like(grad_out)

    for part in range(BLOCK // SUB):
        lanes = slice(part * SUB, (part + 1) * SUB)
        position = step * BLOCK + part * SUB + lax.broadcasted_iota(jnp.int32, (1, SUB), 1)
        live = jnp.where(position < count[0], 1.0, 0.0).astype(F32)
        edges_t = edges[:, lanes] if last else edges[lanes, :].T
        new_edges, added = edge_step(
            edges_t, src[:, lanes], dst[:, lanes], live, iota[...], kv_t, q_t, we_t
        )
        summed[...] += added
        if not last:
            out_edges[:, lanes] = new_edges
            continue
        act = nn(head_in_t[...], new_edges)
        sig = sigmoid(act)
        hidden = (act * sig).astype(BF16)
        pred = nn(head_out_t[...], hidden)
        dpred = (live * (pred - targets[:, lanes].astype(F32)) * scale).astype(BF16)
        dhidden = nn(head_out[...], dpred)
        dact = (dhidden * sig * (1.0 + act * (1.0 - sig))).astype(BF16)
        grad_in[...] += nt(new_edges, dact)
        grad_out[...] += nt(hidden, dpred)

    @pl.when(step == pl.num_programs(0) - 1)
    def _():
        out_nodes[...] = update_nodes(nodes[...], summed[...], gains[layer : layer + 1, :])


def run_layer(layer, scale, count, nodes, ghosts, w_qkv, w_edge, gains, edges, src, dst, heads):
    atoms, width = nodes.shape
    slots = src.shape[1]
    last = scale is not None
    whole = lambda a: pl.BlockSpec(a.shape, lambda i: (0,) * a.ndim)
    by_layer = lambda a: pl.BlockSpec((1,) + a.shape[1:], lambda i: (layer, 0, 0))
    lanes = lambda rows: pl.BlockSpec((rows, BLOCK), lambda i: (0, i))
    edge_spec = lanes(width) if last else pl.BlockSpec((BLOCK, width), lambda i: (i, 0))
    in_specs = [
        pl.BlockSpec(memory_space=pltpu.SMEM),
        whole(nodes),
        whole(ghosts),
        by_layer(w_qkv),
        by_layer(w_edge),
        whole(gains),
        edge_spec,
        lanes(1),
        lanes(1),
    ]
    out_shape = [jax.ShapeDtypeStruct(nodes.shape, BF16)]
    out_specs = [pl.BlockSpec((atoms, width), lambda i: (0, 0))]
    table_rows = atoms + ghosts.shape[0]
    scratch = [
        pltpu.VMEM((2 * width, table_rows), BF16),
        pltpu.VMEM((width, atoms), BF16),
        pltpu.VMEM((width, width), BF16),
        pltpu.VMEM((256, SUB), BF16),
        pltpu.VMEM((width, atoms), F32),
    ]
    operands = [count, nodes, ghosts, w_qkv, w_edge, gains, edges, src, dst]
    if last:
        head_in, head_out, targets = heads
        operands += list(heads)
        in_specs += [whole(head_in), whole(head_out), lanes(targets.shape[0])]
        for like in (head_in, head_out):
            out_shape.append(jax.ShapeDtypeStruct(like.shape, F32))
            out_specs.append(whole(like))
        scratch += [
            pltpu.VMEM(head_in.shape[::-1], BF16),
            pltpu.VMEM(head_out.shape[::-1], BF16),
        ]
    else:
        out_shape.append(jax.ShapeDtypeStruct((width, slots), BF16))
        out_specs.append(lanes(width))
    return pl.pallas_call(
        functools.partial(layer_kernel, layer, scale),
        grid=(slots // BLOCK,),
        in_specs=in_specs,
        out_specs=out_specs,
        out_shape=out_shape,
        scratch_shapes=scratch,
        compiler_params=pltpu.CompilerParams(
            dimension_semantics=("arbitrary",), vmem_limit_bytes=48 << 20
        ),
    )(*operands)


def with_halo(x, sides, width):
    for axis, dim in sides:
        count, length = (lax.axis_size(axis), x.shape[dim])
        up = [(i, (i + 1) % count) for i in range(count)]
        down = [(j, i) for i, j in up]
        last = lax.slice_in_dim(x, length - width, length, axis=dim)
        initial = lax.slice_in_dim(x, 0, width, axis=dim)
        before = lax.ppermute(last, axis, up)
        after = lax.ppermute(initial, axis, down)
        x = jnp.concatenate([before, x, after], axis=dim)
    return x


def exchange(nodes, corner_index):
    padded = with_halo(nodes[corner_index], (("gx", 0), ("gy", 1)), 1)
    return jnp.concatenate([padded[i, j] for i, j in CELLS], axis=0)


def body(
    node_feat,
    edge_feat,
    edge_src,
    edge_dst,
    edge_count,
    send_idx,
    w_qkv,
    w_edge,
    gains,
    head_in,
    head_out,
    targets,
):
    slots = edge_feat.shape[0]
    layers = w_qkv.shape[0]
    corner_index = send_idx.reshape(2, 2, send_idx.shape[-1])
    src = edge_src.reshape(1, slots)
    dst = edge_dst.reshape(1, slots)
    scale = 0.125 / (slots * lax.axis_size(("rep", "gx", "gy"))) ** 0.5
    nodes = node_feat
    edges = edge_feat
    for layer in range(layers):
        ghosts = exchange(nodes, corner_index)
        last = layer == layers - 1
        outs = run_layer(
            layer,
            scale if last else None,
            edge_count,
            nodes,
            ghosts,
            w_qkv,
            w_edge,
            gains,
            edges,
            src,
            dst,
            (head_in, head_out, targets),
        )
        if last:
            nodes, grad_in, grad_out = outs
        else:
            nodes, edges = outs
    grad_in, grad_out = lax.psum((grad_in, grad_out), ("rep", "gx", "gy"))
    return (nodes, grad_in, grad_out)


def solution(mesh):
    tiles = ("rep", "gx", "gy")
    return jax.shard_map(
        body,
        mesh=mesh,
        in_specs=(
            P(tiles, None),
            P(tiles, None),
            P(tiles),
            P(tiles),
            P(tiles),
            P("rep", "gx", "gy", None, None, None),
            P(),
            P(),
            P(),
            P(),
            P(),
            P(None, tiles),
        ),
        out_specs=(P(tiles, None), P(), P()),
        check_vma=False,
    )
```

```python
import functools

import jax
import jax.numpy as jnp
from jax import lax
from jax.experimental import pallas as pl
from jax.experimental.pallas import tpu as pltpu
from jax.sharding import PartitionSpec as P

F32 = jnp.float32
BF16 = jnp.bfloat16
BLOCK = 1024
SUB = 512
CELLS = tuple((i, j) for i in range(4) for j in range(4) if not (i in (1, 2) and j in (1, 2)))
NT = (((1,), (1,)), ((), ()))


def nn(a, b):
    return jnp.dot(a, b, preferred_element_type=F32)


def nt(a, b):
    return lax.dot_general(a, b, NT, preferred_element_type=F32)


def sigmoid(v):
    return 0.5 * jnp.tanh(0.5 * v) + 0.5


def hot(rows_iota, row, base):
    picked = jnp.where((row >= base) & (row < base + 256), row - base, -1)
    picked = picked.astype(F32).astype(BF16)
    return jnp.where(rows_iota == picked, jnp.ones((), BF16), jnp.zeros((), BF16))


def fill_tables(nodes, ghosts, w_qkv, kv_t, q_t):
    atoms = nodes.shape[0]
    w_t = w_qkv.T
    q_t[...] = nt(w_t[:256], nodes).astype(BF16)
    kv_t[:, :atoms] = nt(w_t[256:], nodes).astype(BF16)
    kv_t[:, atoms:] = nt(w_t[256:], ghosts).astype(BF16)


def edge_step(edges_t, src, dst, live, iota, kv_t, q_t, we_t):
    dst_hot = hot(iota, dst, 0)
    table_rows = kv_t.shape[1]
    gathered = nn(kv_t[:, :256], hot(iota, src, 0))
    for base in range(256, table_rows, 256):
        gathered = gathered + nn(kv_t[:, base : base + 256], hot(iota, src, base))
    pre = gathered[:256] + nn(q_t[...], dst_hot) + nn(we_t[...], edges_t)
    gate = live * sigmoid(pre)
    new_edges = (edges_t.astype(F32) + gate * pre).astype(BF16)
    weighted = gate * gathered[256:]
    high = weighted.astype(BF16)
    low = (weighted - high.astype(F32)).astype(BF16)
    added = nt(jnp.concatenate([high, low], axis=0), dst_hot)
    return new_edges, added[:256] + added[256:]


def update_nodes(nodes, summed_t, gain):
    summed = summed_t.T
    centre = summed - jnp.mean(summed, axis=-1, keepdims=True)
    spread = jnp.mean(centre * centre, axis=-1, keepdims=True)
    return (nodes.astype(F32) + gain * (centre * lax.rsqrt(spread + 1e-05))).astype(BF16)


def layer_kernel(
    layer, scale, count, nodes, ghosts, w_qkv, w_edge, gains, edges, src, dst, *rest
):
    last = scale is not None
    if last:
        head_in, head_out, targets, out_nodes, grad_in, grad_out = rest[:6]
        kv_t, q_t, we_t, iota, summed, head_in_t, head_out_t = rest[6:]
    else:
        out_nodes, out_edges = rest[:2]
        kv_t, q_t, we_t, iota, summed = rest[2:]
    step = pl.program_id(0)

    @pl.when(step == 0)
    def _():
        fill_tables(nodes[...], ghosts[...], w_qkv[0], kv_t, q_t)
        we_t[...] = w_edge[0].T
        iota[...] = lax.broadcasted_iota(jnp.int32, iota.shape, 0).astype(F32).astype(BF16)
        summed[...] = jnp.zeros_like(summed)
        if last:
            head_in_t[...] = head_in[...].T
            head_out_t[...] = head_out[...].T
            grad_in[...] = jnp.zeros_like(grad_in)
            grad_out[...] = jnp.zeros_like(grad_out)

    for part in range(BLOCK // SUB):
        lanes = slice(part * SUB, (part + 1) * SUB)
        position = step * BLOCK + part * SUB + lax.broadcasted_iota(jnp.int32, (1, SUB), 1)
        live = jnp.where(position < count[0], 1.0, 0.0).astype(F32)
        edges_t = edges[:, lanes] if last else edges[lanes, :].T
        new_edges, added = edge_step(
            edges_t, src[:, lanes], dst[:, lanes], live, iota[...], kv_t, q_t, we_t
        )
        summed[...] += added
        if not last:
            out_edges[:, lanes] = new_edges
            continue
        act = nn(head_in_t[...], new_edges)
        sig = sigmoid(act)
        hidden = (act * sig).astype(BF16)
        pred = nn(head_out_t[...], hidden)
        dpred = (live * (pred - targets[:, lanes].astype(F32)) * scale).astype(BF16)
        dhidden = nn(head_out[...], dpred)
        dact = (dhidden * sig * (1.0 + act * (1.0 - sig))).astype(BF16)
        grad_in[...] += nt(new_edges, dact)
        grad_out[...] += nt(hidden, dpred)

    @pl.when(step == pl.num_programs(0) - 1)
    def _():
        out_nodes[...] = update_nodes(nodes[...], summed[...], gains[layer : layer + 1, :])


def run_layer(layer, scale, count, nodes, ghosts, w_qkv, w_edge, gains, edges, src, dst, heads):
    atoms, width = nodes.shape
    slots = src.shape[1]
    last = scale is not None
    whole = lambda a: pl.BlockSpec(a.shape, lambda i: (0,) * a.ndim)
    by_layer = lambda a: pl.BlockSpec((1,) + a.shape[1:], lambda i: (layer, 0, 0))
    lanes = lambda rows: pl.BlockSpec((rows, BLOCK), lambda i: (0, i))
    edge_spec = lanes(width) if last else pl.BlockSpec((BLOCK, width), lambda i: (i, 0))
    in_specs = [
        pl.BlockSpec(memory_space=pltpu.SMEM),
        whole(nodes),
        whole(ghosts),
        by_layer(w_qkv),
        by_layer(w_edge),
        whole(gains),
        edge_spec,
        lanes(1),
        lanes(1),
    ]
    out_shape = [jax.ShapeDtypeStruct(nodes.shape, BF16)]
    out_specs = [pl.BlockSpec((atoms, width), lambda i: (0, 0))]
    table_rows = atoms + ghosts.shape[0]
    scratch = [
        pltpu.VMEM((2 * width, table_rows), BF16),
        pltpu.VMEM((width, atoms), BF16),
        pltpu.VMEM((width, width), BF16),
        pltpu.VMEM((256, SUB), BF16),
        pltpu.VMEM((width, atoms), F32),
    ]
    operands = [count, nodes, ghosts, w_qkv, w_edge, gains, edges, src, dst]
    if last:
        head_in, head_out, targets = heads
        operands += list(heads)
        in_specs += [whole(head_in), whole(head_out), lanes(targets.shape[0])]
        for like in (head_in, head_out):
            out_shape.append(jax.ShapeDtypeStruct(like.shape, F32))
            out_specs.append(whole(like))
        scratch += [
            pltpu.VMEM(head_in.shape[::-1], BF16),
            pltpu.VMEM(head_out.shape[::-1], BF16),
        ]
    else:
        out_shape.append(jax.ShapeDtypeStruct((width, slots), BF16))
        out_specs.append(lanes(width))
    return pl.pallas_call(
        functools.partial(layer_kernel, layer, scale),
        grid=(slots // BLOCK,),
        in_specs=in_specs,
        out_specs=out_specs,
        out_shape=out_shape,
        scratch_shapes=scratch,
        compiler_params=pltpu.CompilerParams(
            dimension_semantics=("arbitrary",), vmem_limit_bytes=48 << 20
        ),
    )(*operands)


MESH = pl.DeviceIdType.MESH
HALVES = ((-1, 1), (0, 0), (0, 1), (1, 0))


def greet(devices):
    barrier = pltpu.get_barrier_semaphore()
    for device in devices:
        pl.semaphore_signal(barrier, inc=1, device_id=device, device_id_type=MESH)
    pl.semaphore_wait(barrier, len(devices))


def halo_kernel(sizes, nodes, picks, out, cells, landed, send_sem, recv_sem):
    rep, gx, gy = (lax.axis_index(a) for a in ("rep", "gx", "gy"))

    def at(dx, dy):
        return (rep, lax.rem(gx + sizes[0] + dx, sizes[0]), lax.rem(gy + sizes[1] + dy, sizes[1]))

    offsets = [(i, j) for i in (-1, 0, 1) for j in (-1, 0, 1) if (i, j) != (0, 0)]
    greet([at(i, j) for i, j in offsets])
    atoms = nodes.shape[0]
    rows = lax.broadcasted_iota(jnp.int32, (atoms, picks.shape[1]), 0)
    picked_t = jnp.where(rows == picks[...], 1.0, 0.0).astype(F32)
    cells[...] = nn(picked_t.T.astype(BF16), nodes[...]).astype(BF16).reshape(cells.shape)
    copies = []
    for c, (i, j) in enumerate(CELLS):
        (dx, half_x), (dy, half_y) = HALVES[i], HALVES[j]
        copy = pltpu.make_async_remote_copy(
            src_ref=cells.at[half_x * 2 + half_y],
            dst_ref=landed.at[c],
            send_sem=send_sem.at[c],
            recv_sem=recv_sem.at[c],
            device_id=at(-dx, -dy),
            device_id_type=MESH,
        )
        copy.start()
        copies.append(copy)
    for copy in copies:
        copy.wait()
    out[...] = landed[...].reshape(out.shape)


def exchange(nodes, picks):
    atoms, width = nodes.shape
    cell_rows = picks.shape[1] // 4
    vmem = pl.BlockSpec(memory_space=pltpu.VMEM)
    sizes = (lax.axis_size("gx"), lax.axis_size("gy"))
    return pl.pallas_call(
        functools.partial(halo_kernel, sizes),
        in_specs=[vmem, vmem],
        out_specs=vmem,
        out_shape=jax.ShapeDtypeStruct((len(CELLS) * cell_rows, width), BF16),
        scratch_shapes=[
            pltpu.VMEM((4, cell_rows, width), BF16),
            pltpu.VMEM((len(CELLS), cell_rows, width), BF16),
            pltpu.SemaphoreType.DMA((len(CELLS),)),
            pltpu.SemaphoreType.DMA((len(CELLS),)),
        ],
        compiler_params=pltpu.CompilerParams(collective_id=0, has_side_effects=True),
    )(nodes, picks)


def sum_kernel(sizes, g_in, g_out, s_in, s_out, acc, total, *rest):
    slots, (send_sem, recv_sem) = rest[:-2], rest[-2:]
    rep, gx, gy = (lax.axis_index(a) for a in ("rep", "gx", "gy"))
    n_rep, n_gx, n_gy = sizes
    core, chip = lax.rem(rep, 2), lax.div(rep, 2)
    groups = (
        (2, core, lambda k: (chip * 2 + k, gx, gy)),
        (n_rep // 2, chip, lambda k: (k * 2 + core, gx, gy)),
        (n_gx, gx, lambda k: (rep, k, gy)),
        (n_gy, gy, lambda k: (rep, gx, k)),
    )
    groups = [g for g in groups if g[0] > 1]
    partners = [
        [lax.rem(place + d, count) for d in range(1, count)] for count, place, _ in groups
    ]
    greet([group[2](k) for group, ks in zip(groups, partners) for k in ks])

    parts, rows, lanes = acc.shape
    quarter = parts // 4
    cut = g_out.shape[1] - lanes
    shape = (quarter, rows, lanes)
    acc[:quarter] = g_in[:, :lanes].reshape(shape)
    acc[quarter : 2 * quarter] = g_in[:, lanes:].reshape(shape)
    acc[2 * quarter : 3 * quarter] = g_out[:, :lanes].reshape(shape)
    acc[3 * quarter :] = jnp.pad(g_out[:, lanes:], ((0, 0), (0, lanes - cut))).reshape(shape)

    used = 0

    def send(src, dst, device):
        nonlocal used
        copy = pltpu.make_async_remote_copy(
            src_ref=src,
            dst_ref=dst,
            send_sem=send_sem.at[used],
            recv_sem=recv_sem.at[used],
            device_id=device,
            device_id_type=MESH,
        )
        used += 1
        copy.start()
        return copy

    start, length, ranges = 0, parts, []
    for (count, place, device), ks, slot in zip(groups, partners, slots):
        length //= count
        copies = [
            send(acc.at[pl.ds(start + k * length, length)], slot.at[d], device(k))
            for d, k in enumerate(ks)
        ]
        for copy in copies:
            copy.wait()
        start = start + place * length
        mine = pl.ds(start, length)
        value = acc[mine]
        for d in range(count - 1):
            value = value + slot[d]
        acc[mine] = value
        ranges.append(mine)
    total[ranges[-1]] = acc[ranges[-1]]
    for (count, place, device), ks, mine in reversed(list(zip(groups, partners, ranges))):
        copies = [send(total.at[mine], total.at[mine], device(k)) for k in ks]
        for copy in copies:
            copy.wait()

    flat = (quarter * rows, lanes)
    s_in[:, :lanes] = total[:quarter].reshape(flat)
    s_in[:, lanes:] = total[quarter : 2 * quarter].reshape(flat)
    s_out[:, :lanes] = total[2 * quarter : 3 * quarter].reshape(flat)
    s_out[:, lanes:] = total[3 * quarter :].reshape(flat)[:, :cut]


def sum_all(grad_in, grad_out):
    sizes = tuple(lax.axis_size(a) for a in ("rep", "gx", "gy"))
    lanes = grad_in.shape[1] // 2
    parts = sizes[0] * sizes[1] * sizes[2]
    rows = 4 * grad_in.shape[0] // parts
    counts = [c for c in (2, sizes[0] // 2, sizes[1], sizes[2]) if c > 1]
    slots, length = [], parts
    for count in counts:
        length //= count
        slots.append(pltpu.VMEM((count - 1, length, rows, lanes), F32))
    copies = 2 * sum(c - 1 for c in counts)
    vmem = pl.BlockSpec(memory_space=pltpu.VMEM)
    return pl.pallas_call(
        functools.partial(sum_kernel, sizes),
        in_specs=[vmem, vmem],
        out_specs=[vmem, vmem],
        out_shape=[jax.ShapeDtypeStruct(g.shape, F32) for g in (grad_in, grad_out)],
        scratch_shapes=[
            pltpu.VMEM((parts, rows, lanes), F32),
            pltpu.VMEM((parts, rows, lanes), F32),
            *slots,
            pltpu.SemaphoreType.DMA((copies,)),
            pltpu.SemaphoreType.DMA((copies,)),
        ],
        compiler_params=pltpu.CompilerParams(collective_id=1, has_side_effects=True),
    )(grad_in, grad_out)


def body(
    node_feat,
    edge_feat,
    edge_src,
    edge_dst,
    edge_count,
    send_idx,
    w_qkv,
    w_edge,
    gains,
    head_in,
    head_out,
    targets,
):
    slots = edge_feat.shape[0]
    layers = w_qkv.shape[0]
    picks = send_idx.reshape(1, 4 * send_idx.shape[-1])
    src = edge_src.reshape(1, slots)
    dst = edge_dst.reshape(1, slots)
    scale = 0.125 / (slots * lax.axis_size(("rep", "gx", "gy"))) ** 0.5
    nodes = node_feat
    edges = edge_feat
    for layer in range(layers):
        ghosts = exchange(nodes, picks)
        last = layer == layers - 1
        outs = run_layer(
            layer,
            scale if last else None,
            edge_count,
            nodes,
            ghosts,
            w_qkv,
            w_edge,
            gains,
            edges,
            src,
            dst,
            (head_in, head_out, targets),
        )
        if last:
            nodes, grad_in, grad_out = outs
        else:
            nodes, edges = outs
    grad_in, grad_out = sum_all(grad_in, grad_out)
    return (nodes, grad_in, grad_out)


def solution(mesh):
    tiles = ("rep", "gx", "gy")
    return jax.shard_map(
        body,
        mesh=mesh,
        in_specs=(
            P(tiles, None),
            P(tiles, None),
            P(tiles),
            P(tiles),
            P(tiles),
            P("rep", "gx", "gy", None, None, None),
            P(),
            P(),
            P(),
            P(),
            P(),
            P(None, tiles),
        ),
        out_specs=(P(tiles, None), P(), P()),
        check_vma=False,
    )
```

```python
import functools

import jax
import jax.numpy as jnp
from jax import lax
from jax.experimental import pallas as pl
from jax.experimental.pallas import tpu as pltpu
from jax.sharding import PartitionSpec as P

F32 = jnp.float32
BF16 = jnp.bfloat16
BLOCK = 1024
SUB = 512
CELLS = tuple((i, j) for i in range(4) for j in range(4) if not (i in (1, 2) and j in (1, 2)))
NT = (((1,), (1,)), ((), ()))


def nn(a, b):
    return jnp.dot(a, b, preferred_element_type=F32)


def nt(a, b):
    return lax.dot_general(a, b, NT, preferred_element_type=F32)


def sigmoid(v):
    return 0.5 * jnp.tanh(0.5 * v) + 0.5


def hot(rows_iota, row, base):
    picked = jnp.where((row >= base) & (row < base + 256), row - base, -1)
    picked = picked.astype(F32).astype(BF16)
    return jnp.where(rows_iota == picked, jnp.ones((), BF16), jnp.zeros((), BF16))


def edge_step(edges_t, src, dst, live, iota, kv_t, q_t, we_t):
    dst_hot = hot(iota, dst, 0)
    table_rows = kv_t.shape[1]
    gathered = nn(kv_t[:, :256], hot(iota, src, 0))
    for base in range(256, table_rows, 256):
        gathered = gathered + nn(kv_t[:, base : base + 256], hot(iota, src, base))
    pre = gathered[:256] + nn(q_t[...], dst_hot) + nn(we_t[...], edges_t)
    gate = live * sigmoid(pre)
    new_edges = (edges_t.astype(F32) + gate * pre).astype(BF16)
    weighted = gate * gathered[256:]
    high = weighted.astype(BF16)
    low = (weighted - high.astype(F32)).astype(BF16)
    added = nt(jnp.concatenate([high, low], axis=0), dst_hot)
    return new_edges, added[:256] + added[256:]


def update_nodes(nodes, summed_t, gain):
    summed = summed_t.T
    centre = summed - jnp.mean(summed, axis=-1, keepdims=True)
    spread = jnp.mean(centre * centre, axis=-1, keepdims=True)
    return (nodes.astype(F32) + gain * (centre * lax.rsqrt(spread + 1e-05))).astype(BF16)


MESH = pl.DeviceIdType.MESH
HALVES = ((-1, 1), (0, 0), (0, 1), (1, 0))


def greet(devices):
    barrier = pltpu.get_barrier_semaphore()
    for device in devices:
        pl.semaphore_signal(barrier, inc=1, device_id=device, device_id_type=MESH)
    pl.semaphore_wait(barrier, len(devices))


def whole_kernel(
    sizes,
    layers,
    scale,
    count,
    nodes_in,
    picks,
    w_qkv,
    w_edge,
    gains,
    head_in,
    head_out,
    edges_in,
    src,
    dst,
    targets,
    out_nodes,
    s_in,
    s_out,
    nodes,
    edges,
    kv_t,
    q_t,
    we_t,
    iota,
    summed,
    head_in_t,
    head_out_t,
    g_in,
    g_out,
    cells,
    landed,
    acc,
    total,
    *rest,
):
    slots, (halo_send, halo_recv, sum_send, sum_recv) = rest[:-4], rest[-4:]
    step = pl.program_id(0)
    blocks = edges.shape[0]
    rep, gx, gy = (lax.axis_index(name) for name in ("rep", "gx", "gy"))
    n_rep, n_gx, n_gy = sizes

    def at(dx, dy):
        return (rep, lax.rem(gx + n_gx + dx, n_gx), lax.rem(gy + n_gy + dy, n_gy))

    core, chip = lax.rem(rep, 2), lax.div(rep, 2)
    groups = (
        (2, core, lambda k: (chip * 2 + k, gx, gy)),
        (
            (n_rep // 2) * n_gx,
            chip * n_gx + gx,
            lambda k: (lax.div(k, n_gx) * 2 + core, lax.rem(k, n_gx), gy),
        ),
        (n_gy, gy, lambda k: (rep, gx, k)),
    )
    partners = [
        [lax.rem(place + d, size) for d in range(1, size)] for size, place, _ in groups
    ]

    def send(src_ref, dst_ref, send_sem, recv_sem, device):
        copy = pltpu.make_async_remote_copy(
            src_ref=src_ref,
            dst_ref=dst_ref,
            send_sem=send_sem,
            recv_sem=recv_sem,
            device_id=device,
            device_id_type=MESH,
        )
        copy.start()
        return copy

    def exchange(layer):
        atoms = nodes.shape[0]
        rows = lax.broadcasted_iota(jnp.int32, (atoms, picks.shape[1]), 0)
        picked_t = jnp.where(rows == picks[...], 1.0, 0.0).astype(F32)
        cells[...] = nn(picked_t.T.astype(BF16), nodes[...]).astype(BF16).reshape(cells.shape)
        copies = []
        for c, (i, j) in enumerate(CELLS):
            (dx, half_x), (dy, half_y) = HALVES[i], HALVES[j]
            copies.append(
                send(
                    cells.at[half_x * 2 + half_y],
                    landed.at[layer, c],
                    halo_send.at[layer, c],
                    halo_recv.at[layer, c],
                    at(-dx, -dy),
                )
            )
        w_t = w_qkv[0].T
        q_t[...] = nt(w_t[:256], nodes[...]).astype(BF16)
        kv_t[:, :atoms] = nt(w_t[256:], nodes[...]).astype(BF16)
        we_t[...] = w_edge[0].T
        summed[...] = jnp.zeros_like(summed)
        for copy in copies:
            copy.wait()
        ghosts = landed[layer].reshape(len(CELLS) * cells.shape[1], cells.shape[2])
        kv_t[:, atoms:] = nt(w_t[256:], ghosts).astype(BF16)

    def sum_all():
        parts, rows, lanes = acc.shape
        quarter = parts // 4
        cut = g_out.shape[1] - lanes
        shape = (quarter, rows, lanes)
        acc[:quarter] = g_in[:, :lanes].reshape(shape)
        acc[quarter : 2 * quarter] = g_in[:, lanes:].reshape(shape)
        acc[2 * quarter : 3 * quarter] = g_out[:, :lanes].reshape(shape)
        acc[3 * quarter :] = jnp.pad(g_out[:, lanes:], ((0, 0), (0, lanes - cut))).reshape(shape)
        used, start, length, ranges = 0, 0, parts, []
        for (size, place, device), ks, slot in zip(groups, partners, slots):
            length //= size
            copies = []
            for d, k in enumerate(ks):
                piece = acc.at[pl.ds(start + k * length, length)]
                copies.append(
                    send(piece, slot.at[d], sum_send.at[used], sum_recv.at[used], device(k))
                )
                used += 1
            for copy in copies:
                copy.wait()
            start = start + place * length
            mine = pl.ds(start, length)
            value = acc[mine]
            for d in range(size - 1):
                value = value + slot[d]
            acc[mine] = value
            ranges.append(mine)
        total[ranges[-1]] = acc[ranges[-1]]
        for (size, place, device), ks, mine in reversed(list(zip(groups, partners, ranges))):
            copies = []
            for k in ks:
                piece = total.at[mine]
                copies.append(
                    send(piece, piece, sum_send.at[used], sum_recv.at[used], device(k))
                )
                used += 1
            for copy in copies:
                copy.wait()
        flat = (quarter * rows, lanes)
        s_in[:, :lanes] = total[:quarter].reshape(flat)
        s_in[:, lanes:] = total[quarter : 2 * quarter].reshape(flat)
        s_out[:, :lanes] = total[2 * quarter : 3 * quarter].reshape(flat)
        s_out[:, lanes:] = total[3 * quarter :].reshape(flat)[:, :cut]

    def edge_block(layer, block):
        for part in range(BLOCK // SUB):
            lanes = slice(part * SUB, (part + 1) * SUB)
            position = block * BLOCK + part * SUB + lax.broadcasted_iota(jnp.int32, (1, SUB), 1)
            live = jnp.where(position < count[0], 1.0, 0.0).astype(F32)
            edges_t = edges_in[lanes, :].T if layer == 0 else edges[block, :, lanes]
            new_edges, added = edge_step(
                edges_t, src[:, lanes], dst[:, lanes], live, iota[...], kv_t, q_t, we_t
            )
            summed[...] += added
            if layer < layers - 1:
                edges[block, :, lanes] = new_edges
                continue
            act = nn(head_in_t[...], new_edges)
            sig = sigmoid(act)
            hidden = (act * sig).astype(BF16)
            pred = nn(head_out_t[...], hidden)
            dpred = (live * (pred - targets[:, lanes].astype(F32)) * scale).astype(BF16)
            dhidden = nn(head_out[...], dpred)
            dact = (dhidden * sig * (1.0 + act * (1.0 - sig))).astype(BF16)
            g_in[...] += nt(new_edges, dact)
            g_out[...] += nt(hidden, dpred)

    @pl.when(step == 0)
    def _():
        offsets = [(i, j) for i in (-1, 0, 1) for j in (-1, 0, 1) if (i, j) != (0, 0)]
        greet(
            [at(i, j) for i, j in offsets]
            + [group[2](k) for group, ks in zip(groups, partners) for k in ks]
        )
        nodes[...] = nodes_in[...]
        iota[...] = lax.broadcasted_iota(jnp.int32, iota.shape, 0).astype(F32).astype(BF16)
        head_in_t[...] = head_in[...].T
        head_out_t[...] = head_out[...].T
        g_in[...] = jnp.zeros_like(g_in)
        g_out[...] = jnp.zeros_like(g_out)

    for layer in range(layers):
        first = layer * blocks

        @pl.when(step == first)
        def _():
            exchange(layer)

        @pl.when((step >= first) & (step < first + blocks))
        def _():
            edge_block(layer, step - first)

        @pl.when(step == first + blocks - 1)
        def _():
            nodes[...] = update_nodes(nodes[...], summed[...], gains[layer : layer + 1, :])

    @pl.when(step == layers * blocks - 1)
    def _():
        out_nodes[...] = nodes[...]
        sum_all()


def body(
    node_feat,
    edge_feat,
    edge_src,
    edge_dst,
    edge_count,
    send_idx,
    w_qkv,
    w_edge,
    gains,
    head_in,
    head_out,
    targets,
):
    slots, width = edge_feat.shape
    atoms = node_feat.shape[0]
    layers = w_qkv.shape[0]
    cell_rows = send_idx.shape[-1]
    sizes = tuple(lax.axis_size(name) for name in ("rep", "gx", "gy"))
    devices = sizes[0] * sizes[1] * sizes[2]
    scale = 0.125 / (slots * devices) ** 0.5
    blocks = slots // BLOCK
    lanes = width // 2
    rows = 4 * width // devices
    sum_slots, length, copies = [], devices, 0
    for size in (2, sizes[0] // 2 * sizes[1], sizes[2]):
        length //= size
        copies += 2 * (size - 1)
        sum_slots.append(pltpu.VMEM((size - 1, length, rows, lanes), F32))
    whole = lambda a: pl.BlockSpec(a.shape, lambda i: (0,) * a.ndim)
    by_layer = lambda a: pl.BlockSpec((1,) + a.shape[1:], lambda i: (lax.div(i, blocks), 0, 0))
    row = pl.BlockSpec((1, BLOCK), lambda i: (0, lax.rem(i, blocks)))
    skipped = (layers - 1) * blocks
    picks = send_idx.reshape(1, 4 * cell_rows)
    orb = head_out.shape[1]
    return pl.pallas_call(
        functools.partial(whole_kernel, sizes, layers, scale),
        grid=(layers * blocks,),
        in_specs=[
            pl.BlockSpec(memory_space=pltpu.SMEM),
            whole(node_feat),
            whole(picks),
            by_layer(w_qkv),
            by_layer(w_edge),
            whole(gains),
            whole(head_in),
            whole(head_out),
            pl.BlockSpec((BLOCK, width), lambda i: (jnp.minimum(i, blocks - 1), 0)),
            row,
            row,
            pl.BlockSpec((orb, BLOCK), lambda i: (0, jnp.maximum(i - skipped, 0))),
        ],
        out_specs=[whole(node_feat), whole(head_in), whole(head_out)],
        out_shape=[
            jax.ShapeDtypeStruct(node_feat.shape, BF16),
            jax.ShapeDtypeStruct(head_in.shape, F32),
            jax.ShapeDtypeStruct(head_out.shape, F32),
        ],
        scratch_shapes=[
            pltpu.VMEM((atoms, width), BF16),
            pltpu.VMEM((blocks, width, BLOCK), BF16),
            pltpu.VMEM((2 * width, atoms + len(CELLS) * cell_rows), BF16),
            pltpu.VMEM((width, atoms), BF16),
            pltpu.VMEM((width, width), BF16),
            pltpu.VMEM((256, SUB), BF16),
            pltpu.VMEM((width, atoms), F32),
            pltpu.VMEM(head_in.shape[::-1], BF16),
            pltpu.VMEM(head_out.shape[::-1], BF16),
            pltpu.VMEM(head_in.shape, F32),
            pltpu.VMEM(head_out.shape, F32),
            pltpu.VMEM((4, cell_rows, width), BF16),
            pltpu.VMEM((layers, len(CELLS), cell_rows, width), BF16),
            pltpu.VMEM((devices, rows, lanes), F32),
            pltpu.VMEM((devices, rows, lanes), F32),
            *sum_slots,
            pltpu.SemaphoreType.DMA((layers, len(CELLS))),
            pltpu.SemaphoreType.DMA((layers, len(CELLS))),
            pltpu.SemaphoreType.DMA((copies,)),
            pltpu.SemaphoreType.DMA((copies,)),
        ],
        compiler_params=pltpu.CompilerParams(
            dimension_semantics=("arbitrary",),
            collective_id=0,
            has_side_effects=True,
            vmem_limit_bytes=48 << 20,
        ),
    )(
        edge_count,
        node_feat,
        picks,
        w_qkv,
        w_edge,
        gains,
        head_in,
        head_out,
        edge_feat,
        edge_src.reshape(1, slots),
        edge_dst.reshape(1, slots),
        targets,
    )


def solution(mesh):
    tiles = ("rep", "gx", "gy")
    return jax.shard_map(
        body,
        mesh=mesh,
        in_specs=(
            P(tiles, None),
            P(tiles, None),
            P(tiles),
            P(tiles),
            P(tiles),
            P("rep", "gx", "gy", None, None, None),
            P(),
            P(),
            P(),
            P(),
            P(),
            P(None, tiles),
        ),
        out_specs=(P(tiles, None), P(), P()),
        check_vma=False,
    )
```

```python
import functools

import jax
import jax.numpy as jnp
from jax import lax
from jax.experimental import pallas as pl
from jax.experimental.pallas import tpu as pltpu
from jax.sharding import PartitionSpec as P

F32 = jnp.float32
BF16 = jnp.bfloat16
BLOCK = 1024
SUB = 512
CELLS = tuple((i, j) for i in range(4) for j in range(4) if not (i in (1, 2) and j in (1, 2)))
NT = (((1,), (1,)), ((), ()))


def nn(a, b):
    return jnp.dot(a, b, preferred_element_type=F32)


def nt(a, b):
    return lax.dot_general(a, b, NT, preferred_element_type=F32)


def sigmoid(v):
    return 0.5 * jnp.tanh(0.5 * v) + 0.5


def hot(rows_iota, row, base):
    picked = jnp.where((row >= base) & (row < base + 256), row - base, -1)
    picked = picked.astype(F32).astype(BF16)
    return jnp.where(rows_iota == picked, jnp.ones((), BF16), jnp.zeros((), BF16))


def edge_step(edges_t, src, dst, live, iota, kv_t, q_t, we_t):
    dst_hot = hot(iota, dst, 0)
    table_rows = kv_t.shape[1]
    gathered = nn(kv_t[:, :256], hot(iota, src, 0))
    for base in range(256, table_rows, 256):
        gathered = gathered + nn(kv_t[:, base : base + 256], hot(iota, src, base))
    pre = gathered[:256] + nn(q_t[...], dst_hot) + nn(we_t[...], edges_t)
    gate = live * sigmoid(pre)
    new_edges = (edges_t.astype(F32) + gate * pre).astype(BF16)
    weighted = gate * gathered[256:]
    high = weighted.astype(BF16)
    low = (weighted - high.astype(F32)).astype(BF16)
    added = nt(jnp.concatenate([high, low], axis=0), dst_hot)
    return new_edges, added[:256] + added[256:]


def update_nodes(nodes, summed_t, gain):
    summed = summed_t.T
    centre = summed - jnp.mean(summed, axis=-1, keepdims=True)
    spread = jnp.mean(centre * centre, axis=-1, keepdims=True)
    return (nodes.astype(F32) + gain * (centre * lax.rsqrt(spread + 1e-05))).astype(BF16)


MESH = pl.DeviceIdType.MESH
HALVES = ((-1, 1), (0, 0), (0, 1), (1, 0))


def greet(devices):
    barrier = pltpu.get_barrier_semaphore()
    for device in devices:
        pl.semaphore_signal(barrier, inc=1, device_id=device, device_id_type=MESH)
    pl.semaphore_wait(barrier, len(devices))


def whole_kernel(
    sizes,
    layers,
    scale,
    count,
    nodes_in,
    picks,
    w_qkv,
    w_edge,
    gains,
    head_in,
    head_out,
    edges_in,
    src,
    dst,
    targets,
    out_nodes,
    s_in,
    s_out,
    nodes,
    edges,
    kv_t,
    q_t,
    we_t,
    iota,
    summed,
    head_in_t,
    head_out_t,
    g_in,
    g_out,
    cells,
    landed,
    acc,
    total,
    *rest,
):
    slots, (halo_send, halo_recv, sum_send, sum_recv) = rest[:-4], rest[-4:]
    step = pl.program_id(0)
    blocks = edges.shape[0]
    rep, gx, gy = (lax.axis_index(name) for name in ("rep", "gx", "gy"))
    n_rep, n_gx, n_gy = sizes

    def at(dx, dy):
        return (rep, lax.rem(gx + n_gx + dx, n_gx), lax.rem(gy + n_gy + dy, n_gy))

    core, chip = lax.rem(rep, 2), lax.div(rep, 2)
    groups = (
        (2, core, lambda k: (chip * 2 + k, gx, gy)),
        (
            (n_rep // 2) * n_gx,
            chip * n_gx + gx,
            lambda k: (lax.div(k, n_gx) * 2 + core, lax.rem(k, n_gx), gy),
        ),
        (n_gy, gy, lambda k: (rep, gx, k)),
    )
    partners = [
        [lax.rem(place + d, size) for d in range(1, size)] for size, place, _ in groups
    ]

    def send(src_ref, dst_ref, send_sem, recv_sem, device):
        copy = pltpu.make_async_remote_copy(
            src_ref=src_ref,
            dst_ref=dst_ref,
            send_sem=send_sem,
            recv_sem=recv_sem,
            device_id=device,
            device_id_type=MESH,
        )
        copy.start()
        return copy

    def exchange(layer):
        atoms = nodes.shape[0]
        rows = lax.broadcasted_iota(jnp.int32, (atoms, picks.shape[1]), 0)
        picked_t = jnp.where(rows == picks[...], 1.0, 0.0).astype(F32)
        cells[...] = nn(picked_t.T.astype(BF16), nodes[...]).astype(BF16).reshape(cells.shape)
        copies = []
        for c, (i, j) in enumerate(CELLS):
            (dx, half_x), (dy, half_y) = HALVES[i], HALVES[j]
            copies.append(
                send(
                    cells.at[half_x * 2 + half_y],
                    landed.at[layer, c],
                    halo_send.at[layer, c],
                    halo_recv.at[layer, c],
                    at(-dx, -dy),
                )
            )
        w_t = w_qkv[0].T
        q_t[...] = nt(w_t[:256], nodes[...]).astype(BF16)
        kv_t[:, :atoms] = nt(w_t[256:], nodes[...]).astype(BF16)
        we_t[...] = w_edge[0].T
        summed[...] = jnp.zeros_like(summed)
        for copy in copies:
            copy.wait()
        ghosts = landed[layer].reshape(len(CELLS) * cells.shape[1], cells.shape[2])
        kv_t[:, atoms:] = nt(w_t[256:], ghosts).astype(BF16)

    def sum_all():
        parts, rows, lanes = acc.shape
        quarter = parts // 4
        cut = g_out.shape[1] - lanes
        shape = (quarter, rows, lanes)
        acc[:quarter] = g_in[:, :lanes].reshape(shape)
        acc[quarter : 2 * quarter] = g_in[:, lanes:].reshape(shape)
        acc[2 * quarter : 3 * quarter] = g_out[:, :lanes].reshape(shape)
        acc[3 * quarter :] = jnp.pad(g_out[:, lanes:], ((0, 0), (0, lanes - cut))).reshape(shape)
        used, start, length, ranges = 0, 0, parts, []
        for (size, place, device), ks, slot in zip(groups, partners, slots):
            length //= size
            copies = []
            for d, k in enumerate(ks):
                piece = acc.at[pl.ds(start + k * length, length)]
                copies.append(
                    send(piece, slot.at[d], sum_send.at[used], sum_recv.at[used], device(k))
                )
                used += 1
            for copy in copies:
                copy.wait()
            start = start + place * length
            mine = pl.ds(start, length)
            value = acc[mine]
            for d in range(size - 1):
                value = value + slot[d]
            acc[mine] = value
            ranges.append(mine)
        total[ranges[-1]] = acc[ranges[-1]]
        for (size, place, device), ks, mine in reversed(list(zip(groups, partners, ranges))):
            copies = []
            for k in ks:
                piece = total.at[mine]
                copies.append(
                    send(piece, piece, sum_send.at[used], sum_recv.at[used], device(k))
                )
                used += 1
            for copy in copies:
                copy.wait()
        flat = (quarter * rows, lanes)
        s_in[:, :lanes] = total[:quarter].reshape(flat)
        s_in[:, lanes:] = total[quarter : 2 * quarter].reshape(flat)
        s_out[:, :lanes] = total[2 * quarter : 3 * quarter].reshape(flat)
        s_out[:, lanes:] = total[3 * quarter :].reshape(flat)[:, :cut]

    def edge_block(layer, block):
        for part in range(BLOCK // SUB):
            lanes = slice(part * SUB, (part + 1) * SUB)
            position = block * BLOCK + part * SUB + lax.broadcasted_iota(jnp.int32, (1, SUB), 1)
            live = jnp.where(position < count[0], 1.0, 0.0).astype(F32)
            edges_t = edges_in[lanes, :].T if layer == 0 else edges[block, :, lanes]
            new_edges, added = edge_step(
                edges_t, src[:, lanes], dst[:, lanes], live, iota[...], kv_t, q_t, we_t
            )
            summed[...] += added
            if layer < layers - 1:
                edges[block, :, lanes] = new_edges
                continue
            act = nn(head_in_t[...], new_edges)
            sig = sigmoid(act)
            hidden = (act * sig).astype(BF16)
            pred = nn(head_out_t[...], hidden)
            dpred = (live * (pred - targets[:, lanes].astype(F32)) * scale).astype(BF16)
            dhidden = nn(head_out[...], dpred)
            dact = (dhidden * sig * (1.0 + act * (1.0 - sig))).astype(BF16)
            g_in[...] += nt(new_edges, dact)
            g_out[...] += nt(hidden, dpred)

    @pl.when(step == 0)
    def _():
        offsets = [(i, j) for i in (-1, 0, 1) for j in (-1, 0, 1) if (i, j) != (0, 0)]
        greet(
            [at(i, j) for i, j in offsets]
            + [group[2](k) for group, ks in zip(groups, partners) for k in ks]
        )
        nodes[...] = nodes_in[...]
        iota[...] = lax.broadcasted_iota(jnp.int32, iota.shape, 0).astype(F32).astype(BF16)
        head_in_t[...] = head_in[...].T
        head_out_t[...] = head_out[...].T
        g_in[...] = jnp.zeros_like(g_in)
        g_out[...] = jnp.zeros_like(g_out)

    for layer in range(layers):
        first = layer * blocks

        @pl.when(step == first)
        def _():
            exchange(layer)

        @pl.when((step >= first) & (step < first + blocks))
        def _():
            edge_block(layer, step - first)

        @pl.when(step == first + blocks - 1)
        def _():
            nodes[...] = update_nodes(nodes[...], summed[...], gains[layer : layer + 1, :])

    @pl.when(step == layers * blocks - 1)
    def _():
        out_nodes[...] = nodes[...]
        sum_all()


def body(
    node_feat,
    edge_feat,
    edge_src,
    edge_dst,
    edge_count,
    send_idx,
    w_qkv,
    w_edge,
    gains,
    head_in,
    head_out,
    targets,
):
    slots, width = edge_feat.shape
    atoms = node_feat.shape[0]
    layers = w_qkv.shape[0]
    cell_rows = send_idx.shape[-1]
    sizes = tuple(lax.axis_size(name) for name in ("rep", "gx", "gy"))
    devices = sizes[0] * sizes[1] * sizes[2]
    scale = 0.125 / (slots * devices) ** 0.5
    blocks = slots // BLOCK
    lanes = width // 2
    rows = 4 * width // devices
    sum_slots, length, copies = [], devices, 0
    for size in (2, sizes[0] // 2 * sizes[1], sizes[2]):
        length //= size
        copies += 2 * (size - 1)
        sum_slots.append(pltpu.VMEM((size - 1, length, rows, lanes), F32))
    whole = lambda a: pl.BlockSpec(a.shape, lambda i: (0,) * a.ndim)
    by_layer = lambda a: pl.BlockSpec((1,) + a.shape[1:], lambda i: (lax.div(i, blocks), 0, 0))
    row = pl.BlockSpec((1, BLOCK), lambda i: (0, lax.rem(i, blocks)))
    skipped = (layers - 1) * blocks
    picks = send_idx.reshape(1, 4 * cell_rows)
    orb = head_out.shape[1]
    return pl.pallas_call(
        functools.partial(whole_kernel, sizes, layers, scale),
        grid=(layers * blocks,),
        in_specs=[
            pl.BlockSpec(memory_space=pltpu.SMEM),
            whole(node_feat),
            whole(picks),
            by_layer(w_qkv),
            by_layer(w_edge),
            whole(gains),
            whole(head_in),
            whole(head_out),
            pl.BlockSpec((BLOCK, width), lambda i: (jnp.minimum(i, blocks - 1), 0)),
            row,
            row,
            pl.BlockSpec((orb, BLOCK), lambda i: (0, jnp.maximum(i - skipped, 0))),
        ],
        out_specs=[whole(node_feat), whole(head_in), whole(head_out)],
        out_shape=[
            jax.ShapeDtypeStruct(node_feat.shape, BF16),
            jax.ShapeDtypeStruct(head_in.shape, F32),
            jax.ShapeDtypeStruct(head_out.shape, F32),
        ],
        scratch_shapes=[
            pltpu.VMEM((atoms, width), BF16),
            pltpu.VMEM((blocks, width, BLOCK), BF16),
            pltpu.VMEM((2 * width, atoms + len(CELLS) * cell_rows), BF16),
            pltpu.VMEM((width, atoms), BF16),
            pltpu.VMEM((width, width), BF16),
            pltpu.VMEM((256, SUB), BF16),
            pltpu.VMEM((width, atoms), F32),
            pltpu.VMEM(head_in.shape[::-1], BF16),
            pltpu.VMEM(head_out.shape[::-1], BF16),
            pltpu.VMEM(head_in.shape, F32),
            pltpu.VMEM(head_out.shape, F32),
            pltpu.VMEM((4, cell_rows, width), BF16),
            pltpu.VMEM((layers, len(CELLS), cell_rows, width), BF16),
            pltpu.VMEM((devices, rows, lanes), F32),
            pltpu.VMEM((devices, rows, lanes), F32),
            *sum_slots,
            pltpu.SemaphoreType.DMA((layers, len(CELLS))),
            pltpu.SemaphoreType.DMA((layers, len(CELLS))),
            pltpu.SemaphoreType.DMA((copies,)),
            pltpu.SemaphoreType.DMA((copies,)),
        ],
        compiler_params=pltpu.CompilerParams(
            dimension_semantics=("arbitrary",),
            collective_id=0,
            has_side_effects=True,
            vmem_limit_bytes=60 << 20,
        ),
    )(
        edge_count,
        node_feat,
        picks,
        w_qkv,
        w_edge,
        gains,
        head_in,
        head_out,
        edge_feat,
        edge_src.reshape(1, slots),
        edge_dst.reshape(1, slots),
        targets,
    )


def solution(mesh):
    tiles = ("rep", "gx", "gy")
    return jax.shard_map(
        body,
        mesh=mesh,
        in_specs=(
            P(tiles, None),
            P(tiles, None),
            P(tiles),
            P(tiles),
            P(tiles),
            P("rep", "gx", "gy", None, None, None),
            P(),
            P(),
            P(),
            P(),
            P(),
            P(None, tiles),
        ),
        out_specs=(P(tiles, None), P(), P()),
        check_vma=False,
    )
```
